256 devices in a mesh: rep: 4 (over z_hi), fsdp: 64 (over z_lo, y, x, core).
Axes of the slice: x: 4, y: 4, z: 8 (z_hi: 4, z_lo: 2; z = z_hi * 2 + z_lo), core: 2. Of those that a mesh axis runs over, the one named last changes fastest.
Arguments:
- inputs: bfloat16 [4, 12288, 4096], P('rep', 'fsdp'), may hold values from -16 to 16
- grad_kv: bfloat16 [4, 12288, 1024], P('rep', 'fsdp'), may hold values from -6 to 6
- local_weight: float32 [4, 4096, 1024], P('rep', 'fsdp'), may hold values from -0.09375 to 0.09375
- global_weight: float32 [4096, 1024], P('fsdp'), may hold values from -0.09375 to 0.09375
- outer_moment: float32 [4096, 1024], P('fsdp'), may hold values from -0.15625 to 0.15625
- arrived: float32 [4096, 512], P('fsdp'), may hold values from -0.09375 to 0.09375
- fragment: int32 [1], replicated, may hold values from 0 to 65535
Outputs:
- keys_values: bfloat16 [4, 12288, 1024], P('rep', 'fsdp')
- grad_input: bfloat16 [4, 12288, 4096], P('rep', 'fsdp')
- local_next: float32 [4, 4096, 1024], P('rep', 'fsdp')
- global_next: float32 [4096, 1024], P('fsdp')
- moment_next: float32 [4096, 1024], P('fsdp')
The draws below stay inside these ranges and needn't reach their ends.
Inputs may be any that keep to these rules, and one draw needn't show every extreme that they name: `fragment`: an even number names the key columns, an odd one the value columns.
All inputs are finite; a program needn't handle non-finite values.
Results may differ from the reference program's by a relative error of at most 0.001.
The reference program's roundings to bfloat16 on the way (of `weight_bf`) count: a program that leaves them out, or rounds other values in their place, can miss the bound.
Values may be sent and summed in bfloat16 or wider, within the bound.
A program may use at most 128 MiB of HBM per device.

```python
import jax
import jax.numpy as jnp
from jax import lax

D = 4096
KW = 512
REPS = 4
TOKENS = 12288


def with_spikes(result, stream_key, source, target, parts, factor):
    def block_of(axis_at):
        return (jnp.arange(result.shape[axis_at]) // (result.shape[axis_at] // parts)).reshape((-1,) + (1,) * (result.ndim - 1 - axis_at))

    one_side = jax.random.permutation(stream_key, parts)[block_of(target)]
    second = (block_of(target) + parts // 2) % parts
    return jnp.where((block_of(source) == one_side) | (block_of(source) == second), factor * result, result)


def level_of(rng, shape, split, least, top_value):
    factor_of = 1.0
    for dim, blocks in split:
        steps = jax.random.uniform(jax.random.fold_in(jax.random.fold_in(rng, 6), dim), (blocks,), jnp.float32, least / len(split), top_value / len(split))
        factor_of = factor_of * jnp.repeat(jnp.exp(steps), shape[dim] // blocks).reshape((-1,) + (1,) * (len(shape) - 1 - dim))
    return factor_of


def scatter_about(key, extent, spread, limit, cuts=(), dtype=jnp.bfloat16):
    factor_of = level_of(key, extent, cuts, -0.22, 0.18) if cuts else 1.0
    result = jax.random.normal(key, extent, jnp.float32) * spread * factor_of
    return jnp.minimum(jnp.maximum(result, -limit), limit).astype(dtype)


def bell_draw_with(stream_key, dims, deviation, limit, split, heavy, held_as=jnp.bfloat16):
    entries = deviation * jax.random.normal(stream_key, dims, jnp.float32)
    if split:
        entries = entries * level_of(stream_key, dims, split, -0.22, 0.18)
    return jnp.clip(with_spikes(entries, jax.random.fold_in(stream_key, 3), *heavy), -limit, limit).astype(held_as)


def setup_inputs(seed: int = 0) -> dict:
    streams_of = jax.random.split(jax.random.key(seed), 8)
    inputs = bell_draw_with(streams_of[0], (REPS, TOKENS, D), 1.0, 16.0, ((0, 4), (1, 64)), (1, 2, 64, 4.0))
    grad_kv = scatter_about(streams_of[1], (REPS, TOKENS, 2 * KW), 1.0, 6.0, ((0, 4), (1, 64)))
    local_weight = scatter_about(streams_of[2], (REPS, D, 2 * KW), D ** -0.5, 0.09375, ((0, 4), (1, 64)), jnp.float32)
    global_weight = scatter_about(streams_of[3], (D, 2 * KW), D ** -0.5, 0.09375, ((0, 64),), jnp.float32)
    outer_moment = scatter_about(streams_of[4], (D, 2 * KW), 0.01, 0.15625, ((0, 64),), jnp.float32)
    arrived = scatter_about(streams_of[5], (D, KW), D ** -0.5, 0.09375, ((0, 64),), jnp.float32)
    fragment = jax.random.randint(streams_of[6], (1,), 0, 65536).astype(jnp.int32)
    return dict(inputs=inputs, grad_kv=grad_kv, local_weight=local_weight, global_weight=global_weight, outer_moment=outer_moment, arrived=arrived, fragment=fragment)


inner_rate = 1e-4
outer_rate = 0.7
moment_keep = 0.9
merge_keep = 0.5


def replica_step(items):
    rows, cotangent, weight = items
    weight_bf = weight.astype(jnp.bfloat16)
    produced = jnp.dot(rows, weight_bf, preferred_element_type=jnp.float32).astype(jnp.bfloat16)
    back = lax.dot_general(cotangent, weight_bf, (((1,), (1,)), ((), ())), preferred_element_type=jnp.float32).astype(jnp.bfloat16)
    gradient = lax.dot_general(rows, cotangent, (((0,), (0,)), ((), ())), preferred_element_type=jnp.float32)
    return produced, back, weight - inner_rate * gradient


def reference(inputs, grad_kv, local_weight, global_weight, outer_moment, arrived, fragment):
    keys_values, grad_input, inner = lax.map(replica_step, (inputs, grad_kv, local_weight))
    start = ((fragment[0] % 2) * KW).astype(jnp.int32)
    zero = jnp.int32(0)
    local_part = lax.dynamic_slice_in_dim(local_weight, start, KW, 2)
    global_part = lax.dynamic_slice_in_dim(global_weight, start, KW, 1)
    moment_part = lax.dynamic_slice_in_dim(outer_moment, start, KW, 1)
    mean_delta = jnp.sum(global_part[None] - local_part, axis=0) / REPS
    moment_new = moment_keep * moment_part + mean_delta
    global_new = global_part - outer_rate * (mean_delta + moment_keep * moment_new)
    moment_next = lax.dynamic_update_slice(outer_moment, moment_new, (zero, start))
    global_next = lax.dynamic_update_slice(global_weight, global_new, (zero, start))
    inner_part = lax.dynamic_slice_in_dim(inner, start, KW, 2)
    merged = merge_keep * inner_part + (1.0 - merge_keep) * arrived[None]
    local_next = lax.dynamic_update_slice(inner, merged, (zero, zero, start))
    return keys_values, grad_input, local_next, global_next, moment_next
```

```python
import jax
import jax.numpy as jnp
from jax import lax
from jax.experimental import pallas as pl
from jax.experimental.pallas import tpu as pltpu
from jax.sharding import PartitionSpec as P

inner_rate = 0.0001
outer_rate = 0.7
moment_keep = 0.9
merge_keep = 0.5

MESH = pl.DeviceIdType.MESH
F32, BF16, I16, I32 = jnp.float32, jnp.bfloat16, jnp.int16, jnp.int32
T = 192
D = 4096
KW = 512
H = 256
TOP = 32766.0


def exponent_for(bound):
    return jnp.ceil(8.0 * jnp.log2(jnp.maximum(bound, 1e-30) * (1.0 / TOP)))


def step_of(exponent):
    return jnp.exp2(exponent * 0.125)


def encode(values, inverse):
    return jnp.round(values * inverse).astype(I32).astype(I16)


def decode(codes, step):
    return codes.astype(I32).astype(F32) * step


def kernel(
    fragment, x_hbm, g_hbm, lw_hbm, gw_hbm, om_hbm, ar_hbm,
    kv_hbm, gi_hbm, ln_hbm, gn_hbm, mn_hbm,
    xo, xs, go, gs, gt, lw, gw, om, ar, wa, wb, pt, top,
    a1s, a1r, a2s, a2r, a3s, a3r, acc, kva, gia, kvo, gio,
    gr, gx, dl, dr, lno, gno, mno,
    lsem, ssem, rsem,
):
    r = lax.axis_index("rep")
    f = lax.axis_index("fsdp")
    z, y, x, c = f // 32, (f // 8) % 4, (f // 2) % 4, f % 2

    def dev(z_, y_, x_, c_):
        return (r, ((z_ * 4 + y_) * 4 + x_) * 2 + c_)

    sib = dev(z, y, x, 1 - c)
    ring_id = ((lambda d: dev(z, y, (x + d) % 4, c)), (lambda d: dev(z, (y + d) % 4, x, c)))
    flip = (z, 1 - z)
    direct_id = (
        (lambda dz, d: dev(flip[dz], (y + d) % 4, x, c)),
        (lambda dz, d: dev(flip[dz], y, (x + d) % 4, c)),
    )
    offsets = [(dz, d) for dz in range(2) for d in range(4) if (dz, d) != (0, 0)]
    p = (x, y)
    o = (z * 4 + y, z * 4 + x)
    w = (wa, wb)
    cols = (slice(0, 512), slice(512, 1024))

    def other(g, dz, d):
        return flip[dz] * 4 + ((y, x)[g] + d) % 4

    def chunk(g, o_, p_):
        if g == 0:
            return o_ * 4 + p_
        return (o_ // 4) * 16 + p_ * 4 + o_ % 4

    counts = [0, 0]
    sends = []

    def remote(src, dst, to):
        i = counts[0]
        counts[0] += 1
        cp = pltpu.make_async_remote_copy(
            src_ref=src, dst_ref=dst, send_sem=ssem.at[i], recv_sem=rsem.at[i], device_id=to, device_id_type=MESH
        )
        cp.start()
        sends.append(cp)
        return cp

    def local(src, dst):
        i = counts[1]
        counts[1] += 1
        cp = pltpu.make_async_copy(src, dst, lsem.at[i])
        cp.start()
        return cp

    partners = [sib]
    partners += [direct_id[0](dz, d) for dz, d in offsets]
    partners += [direct_id[1](dz, d) for dz, d in offsets if d != 0]
    partners += [((r + d) % 4, f) for d in (1, 2, 3)]
    barrier = pltpu.get_barrier_semaphore()
    for to in partners:
        pl.semaphore_signal(barrier, inc=1, device_id=to, device_id_type=MESH)

    lw_in = local(lw_hbm.at[0], lw)
    go_in = local(g_hbm.at[0], go)
    Q = D // 4
    xo_in = [local(x_hbm.at[0, :, pl.ds(Q * i, Q)], xo.at[:, pl.ds(Q * i, Q)]) for i in range(4)]
    gw_in = local(gw_hbm, gw)
    om_in = local(om_hbm, om)
    ar_in = local(ar_hbm, ar)

    lw_in.wait()
    wa[x, c, o[0]] = lw[:, 0:512].astype(BF16)
    wb[y, c, o[1]] = lw[:, 512:1024].astype(BF16)
    gw_in.wait()
    first = fragment[0] % 2 == 0
    gsel = jnp.where(first, gw[:, 0:KW], gw[:, KW:])
    dl[...] = gsel - jnp.where(first, lw[:, 0:KW], lw[:, KW:])

    pl.semaphore_wait(barrier, len(partners))

    ag1 = [
        [remote(w[g].at[p[g], c, o[g]], w[g].at[p[g], c, o[g]], direct_id[g](dz, d)) for dz, d in offsets]
        for g in range(2)
    ]
    sib_cols = pl.ds(pl.multiple_of((1 - c) * KW, KW), KW)
    my_cols = pl.ds(pl.multiple_of(c * KW, KW), KW)
    gs_in = remote(g_hbm.at[0, :, sib_cols], gs, sib)
    xs_in = [remote(x_hbm.at[0, :, pl.ds(Q * i, Q)], xs.at[:, pl.ds(Q * i, Q)], sib) for i in range(4)]
    rep_in = [remote(dl, dr.at[d - 1], ((r + d) % 4, f)) for d in (1, 2, 3)]

    go_in.wait()
    gt[:, 0:T] = go[:, my_cols].T
    gs_in.wait_recv()
    gt[:, T:] = gs[...].T
    kva[...] = jnp.zeros_like(kva)
    gia[...] = jnp.zeros_like(gia)
    top[...] = jnp.zeros_like(top)

    ag2 = []
    agd = [{}, {}]
    for g in range(2):
        for cp in ag1[g]:
            cp.wait_recv()
        mine = w[g].at[p[g], c]
        ag2.append([remote(mine, mine, ring_id[g](1)), remote(mine, mine, ring_id[g](3))])
        agd[g][0] = [remote(mine, mine, sib)]

    for i in range(4):
        xo_in[i].wait()
        xs_in[i].wait_recv()

        def block(n, carry):
            lanes = pl.ds(pl.multiple_of(Q * i + n * 256, 256), 256)
            rows = jnp.concatenate([xo[:, lanes], xs[:, lanes]], axis=0)
            part = jnp.dot(gt[...], rows, preferred_element_type=F32)
            pt[8 * i + 2 * n] = part[:, 0:128]
            pt[8 * i + 2 * n + 1] = part[:, 128:256]
            size = jnp.max(jnp.abs(part).reshape(64, 8, 256), axis=0)
            top[...] = jnp.maximum(top[...], jnp.maximum(size[:, 0:128], size[:, 128:256]))
            return carry

        lax.fori_loop(0, 4, block, 0)

    bound0 = jnp.broadcast_to(jnp.max(top[...], axis=(0, 1), keepdims=True), (8, 128))
    e0 = exponent_for(bound0)
    inv0 = step_of(-e0)[0:1]

    def tag(exponent):
        e16 = exponent.astype(I32).astype(I16)
        return jnp.concatenate([e16, e16], axis=0)

    def tag_of(ref_rows):
        e = ref_rows[...].astype(I32).astype(F32)[0:8]
        return e, step_of(e)

    base = (0, H)
    rs1 = []
    for g in range(2):
        pair = []
        for s in range(2):
            buf = a1s.at[g, s]

            def enc1(k, carry, g=g, s=s, buf=buf):
                part = pt[chunk(g, k, (p[g] + 2) % 4), pl.ds(base[g] + 128 * s, 128)]
                buf[pl.ds(pl.multiple_of(k * 128, 128), 128)] = encode(part, inv0)
                return carry

            lax.fori_loop(0, 8, enc1, 0)
            buf[pl.ds(1024, 16)] = tag(e0)
            pair.append(remote(buf, a1r.at[g, s], ring_id[g]((1, 3)[s])))
        rs1.append(pair)

    rs2 = []
    bound2 = []
    for g in range(2):
        pair = []
        for s in range(2):
            rs1[g][s].wait_recv()
            got = a1r.at[g, s]
            buf = a2s.at[g, s]
            _, step1 = tag_of(got.at[pl.ds(1024, 16)])
            e2 = exponent_for(bound0 + step1 * TOP)
            inv2 = step_of(-e2)[0:1]
            step1 = step1[0:1]

            def enc2(k, carry, g=g, s=s, buf=buf, got=got, inv2=inv2, step1=step1):
                at = chunk(g, k, (p[g] + (1, 3)[s]) % 4)
                fed = pt[at, pl.ds(base[g] + 128 * s, 128)] + decode(
                    got[pl.ds(pl.multiple_of(k * 128, 128), 128)], step1
                )
                plain = pt[at, pl.ds(base[g] + 128 * (1 - s), 128)]
                buf[pl.ds(pl.multiple_of(k * 256 + 128 * s, 128), 128)] = encode(fed, inv2)
                buf[pl.ds(pl.multiple_of(k * 256 + 128 * (1 - s), 128), 128)] = encode(plain, inv2)
                return carry

            lax.fori_loop(0, 8, enc2, 0)
            buf[pl.ds(2048, 16)] = tag(e2)
            pair.append(remote(buf, a2r.at[g, s], ring_id[g]((1, 3)[s])))
        rs2.append(pair)

    def multiply(g, place, lo, hi):
        def pairs(k, carry):
            parts = []
            lanes = []
            for j in range(2):
                parts += [w[g][place, 0, 2 * k + j], w[g][place, 1, 2 * k + j]]
                lanes.append(pl.ds(pl.multiple_of(chunk(g, 2 * k + j, place) * 128, 128), 128))
            tile = jnp.concatenate(parts, axis=0)
            rows = jnp.concatenate([xo[:, lanes[0]], xo[:, lanes[1]]], axis=1)
            kva[:, cols[g]] += jnp.dot(rows, tile, preferred_element_type=F32)
            back = lax.dot_general(go[:, cols[g]], tile, (((1,), (1,)), ((), ())), preferred_element_type=F32)
            gia[:, lanes[0]] += back[:, 0:128]
            gia[:, lanes[1]] += back[:, 128:256]
            return carry

        lax.fori_loop(lo, hi, pairs, 0)

    ag3 = []
    for g in range(2):
        pair = []
        for s in range(2):
            ag2[g][s].wait_recv()
            src = (p[g] + (3, 1)[s]) % 4
            half = w[g].at[src, c, pl.ds(4 * s, 4)]
            pair.append(remote(half, half, ring_id[g]((1, 3)[s])))
            whole = w[g].at[src, c]
            agd[g][1 + s] = [remote(whole, whole, sib)]
        ag3.append(pair)

    for g in range(2):
        agd[g][0][0].wait_recv()
        multiply(g, p[g], 0, 4)

    for cp in rep_in:
        cp.wait_recv()
    om_in.wait()
    mean_delta = (dl[...] + dr[0] + dr[1] + dr[2]) * 0.25
    moment_new = moment_keep * jnp.where(first, om[:, 0:KW], om[:, KW:]) + mean_delta
    global_new = gsel - outer_rate * (mean_delta + moment_keep * moment_new)
    for h in range(2):
        sel = first if h == 0 else jnp.logical_not(first)
        mno[:, KW * h : KW * (h + 1)] = jnp.where(sel, moment_new, om[:, KW * h : KW * (h + 1)])
        gno[:, KW * h : KW * (h + 1)] = jnp.where(sel, global_new, gw[:, KW * h : KW * (h + 1)])
    outs = [local(mno, mn_hbm), local(gno, gn_hbm)]

    rs3 = []
    for g in range(2):
        steps = []
        total = bound0
        for s in range(2):
            rs2[g][s].wait_recv()
            _, st = tag_of(a2r.at[g, s, pl.ds(2048, 16)])
            steps.append(st[0:1])
            total = total + st * TOP
        e3 = exponent_for(total)
        inv3 = step_of(-e3)[0:1]
        tag3 = tag(e3)

        def summed(k, g=g, steps=steps):
            rows = pl.ds(pl.multiple_of(k * 256, 256), 256)
            return (
                pt[chunk(g, k, p[g]), pl.ds(base[g], H)]
                + decode(a2r[g, 0, rows], steps[0])
                + decode(a2r[g, 1, rows], steps[1])
            )

        group = []
        for j, (dz, d) in enumerate(offsets):
            a3s[g, j, 0:H] = encode(summed(other(g, dz, d)), inv3)
            a3s[g, j, H:] = tag3
            group.append(remote(a3s.at[g, j], a3r.at[g, j], direct_id[g](dz, d)))
        acc[pl.ds(base[g], H)] = summed(o[g])
        rs3.append(group)

    for g in range(2):
        for s in range(2):
            agd[g][1 + s][0].wait_recv()
            multiply(g, (p[g] + (3, 1)[s]) % 4, 0, 4)

    far = []
    for g in range(2):
        for s in range(2):
            ag3[g][s].wait_recv()
            half = w[g].at[(p[g] + 2) % 4, c, pl.ds(4 * s, 4)]
            far.append(remote(half, half, sib))

    for g in range(2):
        for j, cp in enumerate(rs3[g]):
            cp.wait_recv()
            _, st = tag_of(a3r.at[g, j, pl.ds(H, 16)])
            acc[pl.ds(base[g], H)] += decode(a3r[g, j, 0:H], st[0:1])
    gr[...] = acc[...].T
    gx_in = remote(gr.at[pl.ds(pl.multiple_of((1 - c) * 64, 64), 64)], gx, sib)

    for g in range(2):
        for s in range(2):
            far[2 * g + s].wait_recv()
            multiply(g, (p[g] + 2) % 4, 2 * s, 2 * s + 2)

    kvo[...] = kva[...].astype(BF16)
    gio[...] = gia[...].astype(BF16)
    outs += [local(kvo, kv_hbm.at[0]), local(gio, gi_hbm.at[0])]

    ar_in.wait()
    gx_in.wait_recv()

    def finish(gradient, at, is_first):
        inner = lw[:, at] - inner_rate * gradient
        sel = first if is_first else jnp.logical_not(first)
        merged = merge_keep * inner + (1.0 - merge_keep) * ar[...]
        lno[:, at] = jnp.where(sel, merged, inner)

    here = gr[pl.ds(pl.multiple_of(c * 64, 64), 64)]
    there = gx[...]
    finish(jnp.where(c == 0, here, there), slice(0, KW), True)
    finish(jnp.where(c == 0, there, here), slice(KW, 2 * KW), False)
    outs.append(local(lno, ln_hbm.at[0]))

    for cp in sends:
        cp.wait_send()
    for cp in outs:
        cp.wait()


N_REMOTE = 80
N_LOCAL = 16


def device_step(inputs, grad_kv, local_weight, global_weight, outer_moment, arrived, fragment):
    hbm = pl.BlockSpec(memory_space=pl.ANY)
    R = D // 64
    V = pltpu.VMEM
    return pl.pallas_call(
        kernel,
        out_shape=(
            jax.ShapeDtypeStruct((1, T, 2 * KW), BF16),
            jax.ShapeDtypeStruct((1, T, D), BF16),
            jax.ShapeDtypeStruct((1, R, 2 * KW), F32),
            jax.ShapeDtypeStruct((R, 2 * KW), F32),
            jax.ShapeDtypeStruct((R, 2 * KW), F32),
        ),
        in_specs=[pl.BlockSpec(memory_space=pltpu.SMEM)] + [hbm] * 6,
        out_specs=[hbm] * 5,
        scratch_shapes=[
            V((T, D), BF16), V((T, D), BF16),
            V((T, 2 * KW), BF16), V((T, KW), BF16), V((KW, 2 * T), BF16),
            V((R, 2 * KW), F32), V((R, 2 * KW), F32), V((R, 2 * KW), F32), V((R, KW), F32),
            V((4, 2, 8, R, KW), BF16), V((4, 2, 8, R, KW), BF16),
            V((32, KW, 128), F32), V((8, 128), F32),
            V((2, 2, 1040, 128), I16), V((2, 2, 1040, 128), I16),
            V((2, 2, 2064, 128), I16), V((2, 2, 2064, 128), I16),
            V((2, 7, H + 16, 128), I16), V((2, 7, H + 16, 128), I16),
            V((KW, 128), F32), V((T, 2 * KW), F32), V((T, D), F32),
            V((T, 2 * KW), BF16), V((T, D), BF16),
            V((128, KW), F32), V((R, KW), F32), V((R, KW), F32), V((3, R, KW), F32),
            V((R, 2 * KW), F32), V((R, 2 * KW), F32), V((R, 2 * KW), F32),
            pltpu.SemaphoreType.DMA((N_LOCAL,)),
            pltpu.SemaphoreType.DMA((N_REMOTE,)),
            pltpu.SemaphoreType.DMA((N_REMOTE,)),
        ],
        compiler_params=pltpu.CompilerParams(
            collective_id=0, has_side_effects=True, vmem_limit_bytes=60 * 1024 * 1024
        ),
        name="step",
    )(fragment, inputs, grad_kv, local_weight, global_weight, outer_moment, arrived)


def solution(mesh):
    return jax.shard_map(
        device_step,
        mesh=mesh,
        in_specs=(
            P("rep", "fsdp", None),
            P("rep", "fsdp", None),
            P("rep", "fsdp", None),
            P("fsdp", None),
            P("fsdp", None),
            P("fsdp", None),
            P(),
        ),
        out_specs=(
            P("rep", "fsdp", None),
            P("rep", "fsdp", None),
            P("rep", "fsdp", None),
            P("fsdp", None),
            P("fsdp", None),
        ),
        check_vma=False,
    )
```

```python
import jax
import jax.numpy as jnp
from jax import lax
from jax.experimental import pallas as pl
from jax.experimental.pallas import tpu as pltpu
from jax.sharding import PartitionSpec as P

inner_rate = 0.0001
outer_rate = 0.7
moment_keep = 0.9
merge_keep = 0.5

MESH = pl.DeviceIdType.MESH
F32, BF16, I16, I32 = jnp.float32, jnp.bfloat16, jnp.int16, jnp.int32
T = 192
D = 4096
KW = 512
H = 256
TOP = 32766.0


def exponent_for(bound):
    return jnp.ceil(8.0 * jnp.log2(jnp.maximum(bound, 1e-30) * (1.0 / TOP)))


def step_of(exponent):
    return jnp.exp2(exponent * 0.125)


def encode(values, inverse):
    return jnp.round(values * inverse).astype(I32).astype(I16)


def decode(codes, step):
    return codes.astype(I32).astype(F32) * step


def kernel(
    fragment_hbm, x_hbm, g_hbm, lw_hbm, gw_hbm, om_hbm, ar_hbm,
    kvo, gio, lno, gno, mno,
    xo, xs, go, gs, gt, lw, gw, om, ar, wa, wb, pt, top,
    c1s, c1r, a1os, a1or, a1xs, a1xr, a2os, a2or, a2xs, a2xr, a3s, a3r, a4s, a4r,
    acc, kva, gia,
    gr, gx, dl, ds, dr, fragment,
    lsem, ssem, rsem,
):
    r = lax.axis_index("rep")
    f = lax.axis_index("fsdp")
    z, y, x, c = f // 32, (f // 8) % 4, (f // 2) % 4, f % 2
    zx = 1 - z

    def dev(z_, y_, x_, c_):
        return (r, ((z_ * 4 + y_) * 4 + x_) * 2 + c_)

    sib = dev(z, y, x, 1 - c)
    zid = dev(zx, y, x, c)
    ids = ((lambda d: dev(z, y, (x + d) % 4, c)), (lambda d: dev(z, (y + d) % 4, x, c)))
    ring_id = ids
    line_id = (ids[1], ids[0])
    p = (x, y)
    q = (y, x)
    w = (wa, wb)
    cols = (slice(0, KW), slice(KW, 2 * KW))
    base = (0, H)
    own, oth = pl.ds(4 * z, 4), pl.ds(4 * zx, 4)
    turn = (1, 3)

    def chunk(g, plane, q_, p_):
        return plane * 16 + (q_ * 4 + p_ if g == 0 else p_ * 4 + q_)

    counts = [0, 0]
    sends = []

    def remote(src, dst, to):
        i = counts[0]
        counts[0] += 1
        cp = pltpu.make_async_remote_copy(
            src_ref=src, dst_ref=dst, send_sem=ssem.at[i], recv_sem=rsem.at[i], device_id=to, device_id_type=MESH
        )
        cp.start()
        sends.append(cp)
        return cp

    def same(ref, to):
        return remote(ref, ref, to)

    def local(src, dst):
        i = counts[1]
        counts[1] += 1
        cp = pltpu.make_async_copy(src, dst, lsem.at[i])
        cp.start()
        return cp

    partners = [sib, zid]
    partners += [ids[0](d) for d in (1, 2, 3)] + [ids[1](d) for d in (1, 2, 3)]
    partners += [((r + d) % 4, f) for d in (1, 2, 3)]
    barrier = pltpu.get_barrier_semaphore()
    for to in partners:
        pl.semaphore_signal(barrier, inc=1, device_id=to, device_id_type=MESH)

    lw_in = local(lw_hbm.at[0], lw)
    fragment_in = local(fragment_hbm, fragment)
    go_in = local(g_hbm.at[0], go)
    Q = D // 4
    xo_in = [local(x_hbm.at[0, :, pl.ds(Q * i, Q)], xo.at[:, pl.ds(Q * i, Q)]) for i in range(4)]
    gw_in = local(gw_hbm, gw)
    om_in = local(om_hbm, om)
    ar_in = local(ar_hbm, ar)

    lw_in.wait()
    for g in range(2):
        w[g][p[g], c, 4 * z + q[g]] = lw[:, cols[g]].astype(BF16)

    pl.semaphore_wait(barrier, len(partners))

    N = 3 * KW // 4
    ag0 = [same(w[g].at[p[g], c, 4 * z + q[g], :, 0:N], zid) for g in range(2)]
    ag1 = [[same(w[g].at[p[g], c, 4 * z + q[g]], line_id[g](d)) for d in (1, 2, 3)] for g in range(2)]
    sib_cols = pl.ds(pl.multiple_of((1 - c) * KW, KW), KW)
    my_cols = pl.ds(pl.multiple_of(c * KW, KW), KW)
    gs_in = remote(g_hbm.at[0, :, sib_cols], gs, sib)
    xs_in = [remote(x_hbm.at[0, :, pl.ds(Q * i, Q)], xs.at[:, pl.ds(Q * i, Q)], sib) for i in range(4)]

    def tag(exponent):
        e16 = exponent.astype(I32).astype(I16)
        return jnp.concatenate([e16, e16], axis=0)

    def tag_of(rows):
        e = rows.astype(I32).astype(F32)[0:8]
        return step_of(e)

    def largest(values):
        return jnp.broadcast_to(jnp.max(values, axis=(0, 1), keepdims=True), (8, 128))

    gw_in.wait()
    fragment_in.wait()
    first = fragment[0] % 2 == 0
    gsel = jnp.where(first, gw[:, 0:KW], gw[:, KW:])
    dl[...] = gsel - jnp.where(first, lw[:, 0:KW], lw[:, KW:])
    ed = exponent_for(largest(jnp.abs(dl[...])))
    ds[0:64] = encode(dl[...], jnp.concatenate([step_of(-ed)[0:1]] * 4, axis=1))
    ds[64:80] = jnp.concatenate([tag(ed)] * 4, axis=1)

    go_in.wait()
    gt[:, 0:T] = go[:, my_cols].T
    gs_in.wait_recv()
    gt[:, T:] = gs[...].T
    kva[...] = jnp.zeros_like(kva)
    gia[...] = jnp.zeros_like(gia)
    top[...] = jnp.zeros_like(top)

    ag1x = []
    for g in range(2):
        ag0[g].wait_recv()
        ag1x.append([same(w[g].at[p[g], c, 4 * zx + q[g], :, 0:N], line_id[g](d)) for d in (1, 2, 3)])

    def cross(g, place):
        return same(w[g].at[place, c, own, :, N:KW], zid)

    def share(g, place, plane):
        return same(w[g].at[place, c, plane], sib)

    ag2, ag2x, ag3, ag3x = [], [], [], []
    cz = [{}, {}]
    so = [{}, {}]
    sx = [{}, {}]
    for g in range(2):
        for cp in ag1[g]:
            cp.wait_recv()
        mine = w[g].at[p[g], c, own]
        ag2.append([same(mine, ring_id[g](turn[s])) for s in range(2)])
        cz[g][0] = cross(g, p[g])
        so[g][0] = share(g, p[g], own)

    for i in range(4):
        xo_in[i].wait()
        xs_in[i].wait_recv()

        def block(n, carry):
            lanes = pl.ds(pl.multiple_of(Q * i + n * 256, 256), 256)
            rows = jnp.concatenate([xo[:, lanes], xs[:, lanes]], axis=0)
            part = jnp.dot(gt[...], rows, preferred_element_type=F32)
            pt[8 * i + 2 * n] = part[:, 0:128]
            pt[8 * i + 2 * n + 1] = part[:, 128:256]
            size = jnp.max(jnp.abs(part).reshape(64, 8, 256), axis=0)
            top[...] = jnp.maximum(top[...], jnp.maximum(size[:, 0:128], size[:, 128:256]))
            return carry

        lax.fori_loop(0, 4, block, 0)

    bound0 = largest(top[...])
    e0 = exponent_for(bound0)
    inv0 = step_of(-e0)[0:1]
    tag0 = tag(e0)

    stages = (2, 1, 3, 0)
    c1 = []
    for i, d in enumerate(stages):
        for g in range(2):

            def enc(k, carry, g=g, i=i, d=d):
                part = pt[chunk(g, zx, k, (p[g] + d) % 4), pl.ds(base[g] + 192, 64)]
                c1s[i, pl.ds(pl.multiple_of(256 * g + 64 * k, 64), 64)] = encode(part, inv0)
                return carry

            lax.fori_loop(0, 4, enc, 0)
        c1s[i, 512:528] = tag0
        c1.append(remote(c1s.at[i], c1r.at[i], zid))

    def crossed(i):
        c1[i].wait_recv()
        step = tag_of(c1r[i, 512:528])
        for g in range(2):

            def add(k, carry, g=g):
                at = chunk(g, z, k, (p[g] + stages[i]) % 4)
                rows = pl.ds(pl.multiple_of(256 * g + 64 * k, 64), 64)
                pt[at, pl.ds(base[g] + 192, 64)] += decode(c1r[i, rows], step[0:1])
                return carry

            lax.fori_loop(0, 4, add, 0)
        return step * TOP

    def hop1(g, s, plane, half, buf, dst, inv, mark):
        def enc(k, carry):
            part = pt[chunk(g, plane, k, (p[g] + 2) % 4), pl.ds(base[g] + half * s, half)]
            buf[pl.ds(pl.multiple_of(k * half, half), half)] = encode(part, inv)
            return carry

        lax.fori_loop(0, 4, enc, 0)
        buf[4 * half : 4 * half + 16] = mark
        return remote(buf, dst, ring_id[g](turn[s]))

    rs1x = [[hop1(g, s, zx, 96, a1xs.at[g, s], a1xr.at[g, s], inv0, tag0) for s in range(2)] for g in range(2)]

    for g in range(2):
        for cp in ag1x[g]:
            cp.wait_recv()
        ag2x.append([same(w[g].at[p[g], c, oth, :, 0:N], ring_id[g](turn[s])) for s in range(2)])
        cz[g][0].wait_recv()
        sx[g][0] = share(g, p[g], oth)

    bound_own = bound0 + crossed(0)
    e_own = exponent_for(bound_own)
    inv_own = step_of(-e_own)[0:1]
    tag_own = tag(e_own)
    rs1 = [[hop1(g, s, z, 128, a1os.at[g, s], a1or.at[g, s], inv_own, tag_own) for s in range(2)] for g in range(2)]

    rep_in = [remote(ds, dr.at[d - 1], ((r + d) % 4, f)) for d in (1, 2, 3)]

    def hop2(g, s, plane, half, copy, got, buf, dst, bound):
        copy.wait_recv()
        step = tag_of(got[4 * half : 4 * half + 16])
        e = exponent_for(bound + step * TOP)
        inv = step_of(-e)[0:1]
        step = step[0:1]

        def enc(k, carry):
            at = chunk(g, plane, k, (p[g] + turn[s]) % 4)
            fed = pt[at, pl.ds(base[g] + half * s, half)] + decode(got[pl.ds(pl.multiple_of(k * half, half), half)], step)
            plain = pt[at, pl.ds(base[g] + half * (1 - s), half)]
            buf[pl.ds(pl.multiple_of(2 * k * half + half * s, half), half)] = encode(fed, inv)
            buf[pl.ds(pl.multiple_of(2 * k * half + half * (1 - s), half), half)] = encode(plain, inv)
            return carry

        lax.fori_loop(0, 4, enc, 0)
        buf[8 * half : 8 * half + 16] = tag(e)
        return remote(buf, dst, ring_id[g](turn[s]))

    rs2x = [
        [
            hop2(g, s, zx, 96, rs1x[g][s], a1xr.at[g, s], a2xs.at[g, s], a2xr.at[g, s], bound0)
            for s in range(2)
        ]
        for g in range(2)
    ]

    for g in range(2):
        pair = []
        for s in range(2):
            ag2[g][s].wait_recv()
            src = (p[g] + turn[1 - s]) % 4
            pair.append(same(w[g].at[src, c, pl.ds(4 * z + 2 * s, 2)], ring_id[g](turn[s])))
            cz[g][1 + s] = cross(g, src)
            so[g][1 + s] = share(g, src, own)
        ag3.append(pair)

    crossed(1)
    crossed(2)
    rs2 = [
        [
            hop2(g, s, z, 128, rs1[g][s], a1or.at[g, s], a2os.at[g, s], a2or.at[g, s], bound_own)
            for s in range(2)
        ]
        for g in range(2)
    ]

    for g in range(2):
        pair = []
        for s in range(2):
            ag2x[g][s].wait_recv()
            src = (p[g] + turn[1 - s]) % 4
            pair.append(same(w[g].at[src, c, pl.ds(4 * zx + 2 * s, 2), :, 0:N], ring_id[g](turn[s])))
            cz[g][1 + s].wait_recv()
            sx[g][1 + s] = share(g, src, oth)
        ag3x.append(pair)

    def multiply(g, place, plane, copy):
        copy.wait_recv()
        parts = []
        rows = []
        lanes = []
        for k in range(4):
            parts += [w[g][place, 0, 4 * plane + k], w[g][place, 1, 4 * plane + k]]
            lanes.append(pl.ds(pl.multiple_of(chunk(g, plane, k, place) * 128, 128), 128))
            rows.append(xo[:, lanes[k]])
        tile = jnp.concatenate(parts, axis=0)
        kva[:, cols[g]] += jnp.dot(jnp.concatenate(rows, axis=1), tile, preferred_element_type=F32)
        back = lax.dot_general(go[:, cols[g]], tile, (((1,), (1,)), ((), ())), preferred_element_type=F32)
        for k in range(4):
            gia[:, lanes[k]] += back[:, 128 * k : 128 * (k + 1)]

    for g in range(2):
        multiply(g, p[g], z, so[g][0])
        multiply(g, p[g], zx, sx[g][0])

    crossed(3)
    rs3 = []
    bound_x = []
    for g in range(2):
        steps = []
        total, total_x = bound_own, bound0
        for s in range(2):
            rs2x[g][s].wait_recv()
            st_x = tag_of(a2xr[g, s, 768:784])
            rs2[g][s].wait_recv()
            st = tag_of(a2or[g, s, 1024:1040])
            steps.append((st[0:1], st_x[0:1]))
            total, total_x = total + st * TOP, total_x + st_x * TOP
        bound_x.append(total_x)
        e3 = exponent_for(jnp.maximum(total, total_x))
        inv3 = step_of(-e3)[0:1]
        tag3 = tag(e3)

        def sum_own(k, g=g, steps=steps):
            rows = pl.ds(pl.multiple_of(k * 256, 256), 256)
            return (
                pt[chunk(g, z, k, p[g]), pl.ds(base[g], 256)]
                + decode(a2or[g, 0, rows], steps[0][0])
                + decode(a2or[g, 1, rows], steps[1][0])
            )

        def sum_oth(k, g=g, steps=steps):
            rows = pl.ds(pl.multiple_of(k * 192, 192), 192)
            return (
                pt[chunk(g, zx, k, p[g]), pl.ds(base[g], 192)]
                + decode(a2xr[g, 0, rows], steps[0][1])
                + decode(a2xr[g, 1, rows], steps[1][1])
            )

        group = []
        for d in (1, 2, 3):
            a3s[g, d - 1, 0:256] = encode(sum_own((q[g] + d) % 4), inv3)
            a3s[g, d - 1, 256:448] = encode(sum_oth((q[g] + d) % 4), inv3)
            a3s[g, d - 1, 448:464] = tag3
            group.append(remote(a3s.at[g, d - 1], a3r.at[g, d - 1], line_id[g](d)))
        acc[pl.ds(base[g], 256)] = sum_own(q[g])
        pt[chunk(g, zx, q[g], p[g]), pl.ds(base[g], 192)] = sum_oth(q[g])
        rs3.append(group)

    for g in range(2):
        far = (p[g] + 2) % 4
        for s in range(2):
            ag3[g][s].wait_recv()
        cz[g][3] = cross(g, far)
        so[g][3] = share(g, far, own)

    rs4 = []
    for g in range(2):
        total = bound_x[g]
        steps = []
        for j in range(3):
            rs3[g][j].wait_recv()
            steps.append(tag_of(a3r[g, j, 448:464]))
            total = total + steps[j] * TOP
        e4 = exponent_for(total)
        part = pt[chunk(g, zx, q[g], p[g]), pl.ds(base[g], 192)]
        for j in range(3):
            part = part + decode(a3r[g, j, 256:448], steps[j][0:1])
        a4s[g, 0:192] = encode(part, step_of(-e4)[0:1])
        a4s[g, 192:208] = tag(e4)
        rs4.append(remote(a4s.at[g], a4r.at[g], zid))
        part = acc[pl.ds(base[g], 256)]
        for j in range(3):
            part = part + decode(a3r[g, j, 0:256], steps[j][0:1])
        acc[pl.ds(base[g], 256)] = part

    for g in range(2):
        for s in range(2):
            src = (p[g] + turn[1 - s]) % 4
            multiply(g, src, z, so[g][1 + s])
            multiply(g, src, zx, sx[g][1 + s])

    for g in range(2):
        rs4[g].wait_recv()
        step = tag_of(a4r[g, 192:208])
        acc[pl.ds(base[g], 192)] += decode(a4r[g, 0:192], step[0:1])
    gr[...] = acc[...].T
    gx_in = remote(gr.at[pl.ds(pl.multiple_of((1 - c) * 64, 64), 64)], gx, sib)

    for g in range(2):
        far = (p[g] + 2) % 4
        for s in range(2):
            ag3x[g][s].wait_recv()
        cz[g][3].wait_recv()
        sx[g][3] = share(g, far, oth)

    om_in.wait()
    mean_delta = dl[...]
    for j in range(3):
        rep_in[j].wait_recv()
        step = tag_of(dr[j, 64:80])
        mean_delta = mean_delta + decode(dr[j, 0:64], step[0:1])
    mean_delta = mean_delta * 0.25
    moment_new = moment_keep * jnp.where(first, om[:, 0:KW], om[:, KW:]) + mean_delta
    gsel = jnp.where(first, gw[:, 0:KW], gw[:, KW:])
    global_new = gsel - outer_rate * (mean_delta + moment_keep * moment_new)
    for h in range(2):
        sel = first if h == 0 else jnp.logical_not(first)
        mno[:, cols[h]] = jnp.where(sel, moment_new, om[:, cols[h]])
        gno[:, cols[h]] = jnp.where(sel, global_new, gw[:, cols[h]])

    for g in range(2):
        far = (p[g] + 2) % 4
        multiply(g, far, z, so[g][3])
    for g in range(2):
        far = (p[g] + 2) % 4
        multiply(g, far, zx, sx[g][3])

    kvo[...] = kva[...].astype(BF16)
    gio[...] = gia[...].astype(BF16)

    ar_in.wait()
    gx_in.wait_recv()

    def finish(gradient, at, is_first):
        inner = lw[:, at] - inner_rate * gradient
        sel = first if is_first else jnp.logical_not(first)
        merged = merge_keep * inner + (1.0 - merge_keep) * ar[...]
        lno[:, at] = jnp.where(sel, merged, inner)

    here = gr[pl.ds(pl.multiple_of(c * 64, 64), 64)]
    there = gx[...]
    finish(jnp.where(c == 0, here, there), slice(0, KW), True)
    finish(jnp.where(c == 0, there, here), slice(KW, 2 * KW), False)

    for cp in sends:
        cp.wait_send()
    assert counts[0] <= N_REMOTE and counts[1] <= N_LOCAL


def write_out(*refs):
    sem = refs[10]
    copies = [pltpu.make_async_copy(refs[i], refs[5 + i], sem.at[i]) for i in range(5)]
    for cp in copies:
        cp.start()
    for cp in copies:
        cp.wait()


N_REMOTE = 110
N_LOCAL = 16


def device_step(inputs, grad_kv, local_weight, global_weight, outer_moment, arrived, fragment):
    hbm = pl.BlockSpec(memory_space=pltpu.HBM)
    vmem = pl.BlockSpec(memory_space=pltpu.VMEM)
    R = D // 64
    V = pltpu.VMEM
    shapes = (((T, 2 * KW), BF16), ((T, D), BF16), ((R, 2 * KW), F32), ((R, 2 * KW), F32), ((R, 2 * KW), F32))
    held = pl.pallas_call(
        kernel,
        out_shape=tuple(V(shape, dtype) for shape, dtype in shapes),
        in_specs=[hbm] * 7,
        out_specs=[vmem] * 5,
        scratch_shapes=[
            V((T, D), BF16), V((T, D), BF16),
            V((T, 2 * KW), BF16), V((T, KW), BF16), V((KW, 2 * T), BF16),
            V((R, 2 * KW), F32), V((R, 2 * KW), F32), V((R, 2 * KW), F32), V((R, KW), F32),
            V((4, 2, 8, R, KW), BF16), V((4, 2, 8, R, KW), BF16),
            V((32, KW, 128), F32), V((8, 128), F32),
            V((4, 528, 128), I16), V((4, 528, 128), I16),
            V((2, 2, 528, 128), I16), V((2, 2, 528, 128), I16),
            V((2, 2, 400, 128), I16), V((2, 2, 400, 128), I16),
            V((2, 2, 1040, 128), I16), V((2, 2, 1040, 128), I16),
            V((2, 2, 784, 128), I16), V((2, 2, 784, 128), I16),
            V((2, 3, 464, 128), I16), V((2, 3, 464, 128), I16),
            V((2, 208, 128), I16), V((2, 208, 128), I16),
            V((KW, 128), F32), V((T, 2 * KW), F32), V((T, D), F32),
            V((128, KW), F32), V((R, KW), F32), V((R, KW), F32),
            V((R + 16, KW), I16), V((3, R + 16, KW), I16),
            pltpu.SMEM((1,), I32),
            pltpu.SemaphoreType.DMA((N_LOCAL,)),
            pltpu.SemaphoreType.DMA((N_REMOTE,)),
            pltpu.SemaphoreType.DMA((N_REMOTE,)),
        ],
        compiler_params=pltpu.CompilerParams(
            collective_id=0, has_side_effects=True, vmem_limit_bytes=60 * 1024 * 1024
        ),
        name="step",
    )(fragment, inputs, grad_kv, local_weight, global_weight, outer_moment, arrived)
    kv, gi, ln, gn, mn = pl.pallas_call(
        write_out,
        out_shape=tuple(jax.ShapeDtypeStruct(shape, dtype) for shape, dtype in shapes),
        in_specs=[vmem] * 5,
        out_specs=[hbm] * 5,
        scratch_shapes=[pltpu.SemaphoreType.DMA((5,))],
        compiler_params=pltpu.CompilerParams(vmem_limit_bytes=1024 * 1024),
        name="write",
    )(*(pltpu.with_memory_space_constraint(a, pltpu.VMEM) for a in held))
    return kv[None], gi[None], ln[None], gn, mn


def solution(mesh):
    return jax.shard_map(
        device_step,
        mesh=mesh,
        in_specs=(
            P("rep", "fsdp", None),
            P("rep", "fsdp", None),
            P("rep", "fsdp", None),
            P("fsdp", None),
            P("fsdp", None),
            P("fsdp", None),
            P(),
        ),
        out_specs=(
            P("rep", "fsdp", None),
            P("rep", "fsdp", None),
            P("rep", "fsdp", None),
            P("fsdp", None),
            P("fsdp", None),
        ),
        check_vma=False,
    )
```

```python
import jax
import jax.numpy as jnp
from jax import lax
from jax.experimental import pallas as pl
from jax.experimental.pallas import tpu as pltpu
from jax.sharding import PartitionSpec as P

inner_rate = 0.0001
outer_rate = 0.7
moment_keep = 0.9
merge_keep = 0.5

MESH = pl.DeviceIdType.MESH
F32, BF16, I16, I32 = jnp.float32, jnp.bfloat16, jnp.int16, jnp.int32
T = 192
D = 4096
KW = 512
H = 256
TOP = 32766.0


def exponent_for(bound):
    return jnp.ceil(8.0 * jnp.log2(jnp.maximum(bound, 1e-30) * (1.0 / TOP)))


def step_of(exponent):
    return jnp.exp2(exponent * 0.125)


def encode(values, inverse):
    return jnp.round(values * inverse).astype(I32).astype(I16)


def decode(codes, step):
    return codes.astype(I32).astype(F32) * step


def kernel(
    fragment_hbm, x_hbm, g_hbm, lw_hbm, gw_hbm, om_hbm, ar_hbm,
    kvo, gio, lno, gno, mno,
    xo, xs, go, gs, gt, lw, gw, om, ar, wa, wb, pt, top,
    c1s, c1r, a1os, a1or, a1xs, a1xr, a2os, a2or, a2xs, a2xr, a3os, a3or, a3xs, a3xr, a4s, a4r,
    acc, kva, gia,
    gr, gx, dl, ds, dr, fragment,
    lsem, ssem, rsem,
):
    r = lax.axis_index("rep")
    f = lax.axis_index("fsdp")
    z, y, x, c = f // 32, (f // 8) % 4, (f // 2) % 4, f % 2
    zx = 1 - z

    def dev(z_, y_, x_, c_):
        return (r, ((z_ * 4 + y_) * 4 + x_) * 2 + c_)

    sib = dev(z, y, x, 1 - c)
    zid = dev(zx, y, x, c)
    ids = ((lambda d: dev(z, y, (x + d) % 4, c)), (lambda d: dev(z, (y + d) % 4, x, c)))
    ring_id = ids
    line_id = (ids[1], ids[0])
    p = (x, y)
    q = (y, x)
    w = (wa, wb)
    cols = (slice(0, KW), slice(KW, 2 * KW))
    base = (0, H)
    own, oth = pl.ds(4 * z, 4), pl.ds(4 * zx, 4)
    turn = (1, 3)

    def chunk(g, plane, q_, p_):
        return plane * 16 + (q_ * 4 + p_ if g == 0 else p_ * 4 + q_)

    counts = [0, 0]
    sends = []

    def remote(src, dst, to):
        i = counts[0]
        counts[0] += 1
        cp = pltpu.make_async_remote_copy(
            src_ref=src, dst_ref=dst, send_sem=ssem.at[i], recv_sem=rsem.at[i], device_id=to, device_id_type=MESH
        )
        cp.start()
        sends.append(cp)
        return cp

    def same(ref, to):
        return remote(ref, ref, to)

    def local(src, dst):
        i = counts[1]
        counts[1] += 1
        cp = pltpu.make_async_copy(src, dst, lsem.at[i])
        cp.start()
        return cp

    partners = [sib, zid]
    partners += [ids[0](d) for d in (1, 2, 3)] + [ids[1](d) for d in (1, 2, 3)]
    partners += [((r + d) % 4, f) for d in (1, 2, 3)]
    barrier = pltpu.get_barrier_semaphore()
    for to in partners:
        pl.semaphore_signal(barrier, inc=1, device_id=to, device_id_type=MESH)

    lw_in = local(lw_hbm.at[0], lw)
    lw_in.wait()
    Q = D // 4
    go_in = local(g_hbm.at[0], go)
    xo_in = [local(x_hbm.at[0, :, pl.ds(Q * i, Q)], xo.at[:, pl.ds(Q * i, Q)]) for i in range(4)]
    gw_in = local(gw_hbm, gw)
    om_in = local(om_hbm, om)
    ar_in = local(ar_hbm, ar)
    fragment_in = local(fragment_hbm, fragment)
    for g in range(2):
        w[g][p[g], c, 4 * z + q[g]] = lw[:, cols[g]].astype(BF16)

    pl.semaphore_wait(barrier, len(partners))

    N = 3 * KW // 4
    sib_cols = pl.ds(pl.multiple_of((1 - c) * KW, KW), KW)
    my_cols = pl.ds(pl.multiple_of(c * KW, KW), KW)
    both = range(2)

    def tag(exponent):
        e16 = exponent.astype(I32).astype(I16)
        return jnp.concatenate([e16, e16], axis=0)

    def tag_of(rows):
        return step_of(rows.astype(I32).astype(F32)[0:8])

    def scale_of(bound):
        e = exponent_for(bound)
        return step_of(-e)[0:1], tag(e)

    def largest(values):
        return jnp.broadcast_to(jnp.max(values, axis=(0, 1), keepdims=True), (8, 128))

    def bound_of(g, plane, place):
        tops = [top[chunk(g, plane, k, place)] for k in range(4)]
        return largest(jnp.maximum(jnp.maximum(tops[0], tops[1]), jnp.maximum(tops[2], tops[3])))

    ag0, ag1, ag1x, ag2, ag2x, ag3, ag3x = ([None, None] for _ in range(7))
    cz, so, sx = ([{}, {}] for _ in range(3))

    def cross(g, place):
        return same(w[g].at[place, c, own, :, N:KW], zid)

    def share(g, place, plane):
        return same(w[g].at[place, c, plane], sib)

    def source(g, s):
        return (p[g] + turn[1 - s]) % 4

    def gather_z():
        for g in both:
            ag0[g] = same(w[g].at[p[g], c, 4 * z + q[g], :, 0:N], zid)

    def gather_line():
        for g in both:
            ag1[g] = [same(w[g].at[p[g], c, 4 * z + q[g]], line_id[g](d)) for d in (1, 2, 3)]

    def gather_line_x():
        for g in both:
            ag0[g].wait_recv()
            ag1x[g] = [same(w[g].at[p[g], c, 4 * zx + q[g], :, 0:N], line_id[g](d)) for d in (1, 2, 3)]

    def gather_ring():
        for g in both:
            for cp in ag1[g]:
                cp.wait_recv()
            ag2[g] = [same(w[g].at[p[g], c, own], ring_id[g](turn[s])) for s in both]

    def gather_ring_cross():
        for g in both:
            cz[g][0] = cross(g, p[g])
            so[g][0] = share(g, p[g], own)

    def gather_ring_x():
        for g in both:
            for cp in ag1x[g]:
                cp.wait_recv()
            ag2x[g] = [same(w[g].at[p[g], c, oth, :, 0:N], ring_id[g](turn[s])) for s in both]

    def gather_ring_x_share():
        for g in both:
            cz[g][0].wait_recv()
            sx[g][0] = share(g, p[g], oth)

    def gather_far():
        for g in both:
            ag3[g] = []
            for s in both:
                ag2[g][s].wait_recv()
                src = source(g, s)
                ag3[g].append(same(w[g].at[src, c, pl.ds(4 * z + 2 * s, 2)], ring_id[g](turn[s])))

    def gather_far_cross():
        for g in both:
            for s in both:
                cz[g][1 + s] = cross(g, source(g, s))
                so[g][1 + s] = share(g, source(g, s), own)

    def gather_far_x():
        for g in both:
            ag3x[g] = []
            for s in both:
                ag2x[g][s].wait_recv()
                src = source(g, s)
                ag3x[g].append(same(w[g].at[src, c, pl.ds(4 * zx + 2 * s, 2), :, 0:N], ring_id[g](turn[s])))

    def gather_far_x_share():
        for g in both:
            for s in both:
                cz[g][1 + s].wait_recv()
                sx[g][1 + s] = share(g, source(g, s), oth)

    def gather_end():
        for g in both:
            for s in both:
                ag3[g][s].wait_recv()
            cz[g][3] = cross(g, (p[g] + 2) % 4)
            so[g][3] = share(g, (p[g] + 2) % 4, own)

    def gather_end_x():
        for g in both:
            for s in both:
                ag3x[g][s].wait_recv()
            cz[g][3].wait_recv()
            sx[g][3] = share(g, (p[g] + 2) % 4, oth)

    def multiply(g, place, plane, copy):
        copy.wait_recv()
        parts = []
        rows = []
        lanes = []
        for k in range(4):
            parts += [w[g][place, 0, 4 * plane + k], w[g][place, 1, 4 * plane + k]]
            lanes.append(pl.ds(pl.multiple_of(chunk(g, plane, k, place) * 128, 128), 128))
            rows.append(xo[:, lanes[k]])
        tile = jnp.concatenate(parts, axis=0)
        kva[:, cols[g]] += jnp.dot(jnp.concatenate(rows, axis=1), tile, preferred_element_type=F32)
        back = lax.dot_general(go[:, cols[g]], tile, (((1,), (1,)), ((), ())), preferred_element_type=F32)
        for k in range(4):
            gia[:, lanes[k]] += back[:, 128 * k : 128 * (k + 1)]

    def multiply_own():
        for g in both:
            multiply(g, p[g], z, so[g][0])

    def multiply_own_x():
        for g in both:
            multiply(g, p[g], zx, sx[g][0])

    def multiply_near():
        for g in both:
            for s in both:
                multiply(g, source(g, s), z, so[g][1 + s])

    def multiply_near_x():
        for g in both:
            for s in both:
                multiply(g, source(g, s), zx, sx[g][1 + s])

    def multiply_far():
        for g in both:
            multiply(g, (p[g] + 2) % 4, z, so[g][3])

    def multiply_far_x():
        for g in both:
            multiply(g, (p[g] + 2) % 4, zx, sx[g][3])

    ex = {}

    def exchange():
        ex["g"] = remote(g_hbm.at[0, :, sib_cols], gs, sib)
        ex["x"] = [remote(x_hbm.at[0, :, pl.ds(Q * i, Q)], xs.at[:, pl.ds(Q * i, Q)], sib) for i in range(4)]

    def prepare():
        go_in.wait()
        gt[:, 0:T] = go[:, my_cols].T
        ex["g"].wait_recv()
        gt[:, T:] = gs[...].T
        kva[...] = jnp.zeros_like(kva)
        gia[...] = jnp.zeros_like(gia)

    def gradient(*pieces):
        for i in pieces:
            xo_in[i].wait()
            ex["x"][i].wait_recv()

            def block(n, carry):
                lanes = pl.ds(pl.multiple_of(Q * i + n * 256, 256), 256)
                rows = jnp.concatenate([xo[:, lanes], xs[:, lanes]], axis=0)
                part = jnp.dot(gt[...], rows, preferred_element_type=F32)
                pt[8 * i + 2 * n] = part[:, 0:128]
                pt[8 * i + 2 * n + 1] = part[:, 128:256]
                size = jnp.max(jnp.abs(part).reshape(64, 8, 256), axis=0)
                top[8 * i + 2 * n] = size[:, 0:128]
                top[8 * i + 2 * n + 1] = size[:, 128:256]
                return carry

            lax.fori_loop(0, 4, block, 0, unroll=True)

    stages = (2, 1, 3, 0)
    c1, rs1, rs1x, rs2, rs2x, rs3, rs3x, rs4 = ([None] * 4 for _ in range(8))
    extra = [None] * 4

    def cross_rows(i):
        d = stages[i]
        bound = jnp.maximum(bound_of(0, zx, (p[0] + d) % 4), bound_of(1, zx, (p[1] + d) % 4))
        inv, mark = scale_of(bound)
        for g in both:

            def enc(k, carry, g=g):
                part = pt[chunk(g, zx, k, (p[g] + d) % 4), pl.ds(base[g] + 192, 64)]
                c1s[i, pl.ds(pl.multiple_of(256 * g + 64 * k, 64), 64)] = encode(part, inv)
                return carry

            lax.fori_loop(0, 4, enc, 0)
        c1s[i, 512:528] = mark
        c1[i] = remote(c1s.at[i], c1r.at[i], zid)

    def crossed(i):
        c1[i].wait_recv()
        step = tag_of(c1r[i, 512:528])
        for g in both:

            def add(k, carry, g=g):
                at = chunk(g, z, k, (p[g] + stages[i]) % 4)
                rows = pl.ds(pl.multiple_of(256 * g + 64 * k, 64), 64)
                pt[at, pl.ds(base[g] + 192, 64)] += decode(c1r[i, rows], step[0:1])
                return carry

            lax.fori_loop(0, 4, add, 0)
        extra[stages[i]] = step * TOP

    def hop1(g, s, plane, half, buf, dst, more):
        inv, mark = scale_of(bound_of(g, plane, (p[g] + 2) % 4) + more)

        def enc(k, carry):
            part = pt[chunk(g, plane, k, (p[g] + 2) % 4), pl.ds(base[g] + half * s, half)]
            buf[pl.ds(pl.multiple_of(k * half, half), half)] = encode(part, inv)
            return carry

        lax.fori_loop(0, 4, enc, 0)
        buf[4 * half : 4 * half + 16] = mark
        return remote(buf, dst, ring_id[g](turn[s]))

    def scatter1_x():
        for g in both:
            rs1x[g] = [hop1(g, s, zx, 96, a1xs.at[g, s], a1xr.at[g, s], 0.0) for s in both]

    def scatter1():
        for g in both:
            rs1[g] = [hop1(g, s, z, 128, a1os.at[g, s], a1or.at[g, s], extra[2]) for s in both]

    def hop2(g, s, plane, half, copy, got, buf, dst, more):
        copy.wait_recv()
        step = tag_of(got[4 * half : 4 * half + 16])
        inv, mark = scale_of(more + bound_of(g, plane, (p[g] + turn[s]) % 4) + step * TOP)
        step = step[0:1]

        def enc(k, carry):
            at = chunk(g, plane, k, (p[g] + turn[s]) % 4)
            fed = pt[at, pl.ds(base[g] + half * s, half)] + decode(got[pl.ds(pl.multiple_of(k * half, half), half)], step)
            plain = pt[at, pl.ds(base[g] + half * (1 - s), half)]
            buf[pl.ds(pl.multiple_of(2 * k * half + half * s, half), half)] = encode(fed, inv)
            buf[pl.ds(pl.multiple_of(2 * k * half + half * (1 - s), half), half)] = encode(plain, inv)
            return carry

        lax.fori_loop(0, 4, enc, 0)
        buf[8 * half : 8 * half + 16] = mark
        return remote(buf, dst, ring_id[g](turn[s]))

    def scatter2_x():
        for g in both:
            rs2x[g] = [
                hop2(g, s, zx, 96, rs1x[g][s], a1xr.at[g, s], a2xs.at[g, s], a2xr.at[g, s], 0.0) for s in both
            ]

    def scatter2():
        for g in both:
            rs2[g] = [
                hop2(g, s, z, 128, rs1[g][s], a1or.at[g, s], a2os.at[g, s], a2or.at[g, s], extra[turn[s]]) for s in both
            ]

    def hop3(g, plane, rows, copies, got, buf, dst):
        steps = []
        for s in both:
            copies[s].wait_recv()
            steps.append(tag_of(got[s, 4 * rows : 4 * rows + 16])[0:1])
        size = jnp.zeros((8, 128), F32)
        for d in (1, 2, 3, 0):
            k = (q[g] + d) % 4
            part = pl.ds(pl.multiple_of(k * rows, rows), rows)
            at = chunk(g, plane, k, p[g])
            total = pt[at, pl.ds(base[g], rows)] + decode(got[0, part], steps[0]) + decode(got[1, part], steps[1])
            pt[at, pl.ds(base[g], rows)] = total
            if d:
                size = jnp.maximum(size, jnp.max(jnp.abs(total).reshape(rows // 8, 8, 128), axis=0))
        inv, mark = scale_of(largest(size))
        sent = []
        for d in (1, 2, 3):
            at = chunk(g, plane, (q[g] + d) % 4, p[g])
            buf[d - 1, 0:rows] = encode(pt[at, pl.ds(base[g], rows)], inv)
            buf[d - 1, rows : rows + 16] = mark
            sent.append(remote(buf.at[d - 1], dst.at[d - 1], line_id[g](d)))
        return sent

    def scatter3_x():
        for g in both:
            rs3x[g] = hop3(g, zx, 192, rs2x[g], a2xr.at[g], a3xs.at[g], a3xr.at[g])

    def scatter3():
        for g in both:
            rs3[g] = hop3(g, z, 256, rs2[g], a2or.at[g], a3os.at[g], a3or.at[g])

    def scatter4():
        for g in both:
            part = pt[chunk(g, zx, q[g], p[g]), pl.ds(base[g], 192)]
            for j in range(3):
                rs3x[g][j].wait_recv()
                part = part + decode(a3xr[g, j, 0:192], tag_of(a3xr[g, j, 192:208])[0:1])
            inv, mark = scale_of(largest(jnp.abs(part)))
            a4s[g, 0:192] = encode(part, inv)
            a4s[g, 192:208] = mark
            rs4[g] = remote(a4s.at[g], a4r.at[g], zid)

    def scatter_end():
        for g in both:
            part = pt[chunk(g, z, q[g], p[g]), pl.ds(base[g], 256)]
            for j in range(3):
                rs3[g][j].wait_recv()
                part = part + decode(a3or[g, j, 0:256], tag_of(a3or[g, j, 256:272])[0:1])
            acc[pl.ds(base[g], 256)] = part
            rs4[g].wait_recv()
            acc[pl.ds(base[g], 192)] += decode(a4r[g, 0:192], tag_of(a4r[g, 192:208])[0:1])
            gr[:, pl.ds(base[g], 256)] = acc[pl.ds(base[g], 256)].T
        ex["gx"] = remote(gr.at[pl.ds(pl.multiple_of((1 - c) * 64, 64), 64)], gx, sib)

    def is_first():
        return fragment[0] % 2 == 0

    def delta():
        gw_in.wait()
        fragment_in.wait()
        first = is_first()
        dl[...] = jnp.where(first, gw[:, 0:KW] - lw[:, 0:KW], gw[:, KW:] - lw[:, KW:])
        ed = exponent_for(largest(jnp.abs(dl[...])))
        ds[0:64] = encode(dl[...], jnp.concatenate([step_of(-ed)[0:1]] * 4, axis=1))
        ds[64:80] = jnp.concatenate([tag(ed)] * 4, axis=1)

    def replicas():
        ex["rep"] = [remote(ds, dr.at[d - 1], ((r + d) % 4, f)) for d in (1, 2, 3)]

    def outer():
        om_in.wait()
        first = is_first()
        mean_delta = dl[...]
        for j in range(3):
            ex["rep"][j].wait_recv()
            step = tag_of(dr[j, 64:80])
            mean_delta = mean_delta + decode(dr[j, 0:64], step[0:1])
        mean_delta = mean_delta * 0.25
        moment_new = moment_keep * jnp.where(first, om[:, 0:KW], om[:, KW:]) + mean_delta
        global_new = jnp.where(first, gw[:, 0:KW], gw[:, KW:]) - outer_rate * (mean_delta + moment_keep * moment_new)
        for h in both:
            sel = first if h == 0 else jnp.logical_not(first)
            mno[:, cols[h]] = jnp.where(sel, moment_new, om[:, cols[h]])
            gno[:, cols[h]] = jnp.where(sel, global_new, gw[:, cols[h]])

    def half_out(plane):
        lanes = pl.ds(pl.multiple_of(plane * (D // 2), D // 2), D // 2)
        gio[:, lanes] = gia[:, lanes].astype(BF16)

    def products_own():
        half_out(z)

    def products_x():
        half_out(zx)
        kvo[...] = kva[...].astype(BF16)

    def inner_out():
        ar_in.wait()
        ex["gx"].wait_recv()
        first = is_first()
        here = gr[pl.ds(pl.multiple_of(c * 64, 64), 64)]
        there = gx[...]
        for h in both:
            gradient_h = jnp.where(c == h, here, there)
            inner = lw[:, cols[h]] - inner_rate * gradient_h
            sel = first if h == 0 else jnp.logical_not(first)
            merged = merge_keep * inner + (1.0 - merge_keep) * ar[...]
            lno[:, cols[h]] = jnp.where(sel, merged, inner)

    gather_z()
    gather_line()
    exchange()
    delta()
    prepare()
    gather_line_x()
    gather_ring()
    gather_ring_cross()
    gradient(0,1,2,3)
    for i in range(4):
        cross_rows(i)
    scatter1_x()
    gather_ring_x()
    crossed(0)
    scatter1()
    gather_ring_x_share()
    scatter2_x()
    replicas()
    multiply_own()
    crossed(1)
    crossed(2)
    scatter2()
    gather_far()
    gather_far_cross()
    multiply_own_x()
    scatter3_x()
    gather_far_x()
    gather_far_x_share()
    crossed(3)
    scatter3()
    outer()
    multiply_near()
    gather_end()
    scatter4()
    multiply_near_x()
    multiply_far()
    products_own()
    gather_end_x()
    scatter_end()
    multiply_far_x()
    products_x()
    inner_out()

    for cp in sends:
        cp.wait_send()
    assert counts[0] <= N_REMOTE and counts[1] <= N_LOCAL


def write_out(*refs):
    sem = refs[10]
    copies = [pltpu.make_async_copy(refs[i], refs[5 + i], sem.at[i]) for i in range(5)]
    for cp in copies:
        cp.start()
    for cp in copies:
        cp.wait()


N_REMOTE = 120
N_LOCAL = 16


def device_step(inputs, grad_kv, local_weight, global_weight, outer_moment, arrived, fragment):
    hbm = pl.BlockSpec(memory_space=pltpu.HBM)
    vmem = pl.BlockSpec(memory_space=pltpu.VMEM)
    R = D // 64
    V = pltpu.VMEM
    shapes = (((T, 2 * KW), BF16), ((T, D), BF16), ((R, 2 * KW), F32), ((R, 2 * KW), F32), ((R, 2 * KW), F32))
    held = pl.pallas_call(
        kernel,
        out_shape=tuple(V(shape, dtype) for shape, dtype in shapes),
        in_specs=[hbm] * 7,
        out_specs=[vmem] * 5,
        scratch_shapes=[
            V((T, D), BF16), V((T, D), BF16),
            V((T, 2 * KW), BF16), V((T, KW), BF16), V((KW, 2 * T), BF16),
            V((R, 2 * KW), F32), V((R, 2 * KW), F32), V((R, 2 * KW), F32), V((R, KW), F32),
            V((4, 2, 8, R, KW), BF16), V((4, 2, 8, R, KW), BF16),
            V((32, KW, 128), F32), V((32, 8, 128), F32),
            V((4, 528, 128), I16), V((4, 528, 128), I16),
            V((2, 2, 528, 128), I16), V((2, 2, 528, 128), I16),
            V((2, 2, 400, 128), I16), V((2, 2, 400, 128), I16),
            V((2, 2, 1040, 128), I16), V((2, 2, 1040, 128), I16),
            V((2, 2, 784, 128), I16), V((2, 2, 784, 128), I16),
            V((2, 3, 272, 128), I16), V((2, 3, 272, 128), I16),
            V((2, 3, 208, 128), I16), V((2, 3, 208, 128), I16),
            V((2, 208, 128), I16), V((2, 208, 128), I16),
            V((KW, 128), F32), V((T, 2 * KW), F32), V((T, D), F32),
            V((128, KW), F32), V((R, KW), F32), V((R, KW), F32),
            V((R + 16, KW), I16), V((3, R + 16, KW), I16),
            pltpu.SMEM((1,), I32),
            pltpu.SemaphoreType.DMA((N_LOCAL,)),
            pltpu.SemaphoreType.DMA((N_REMOTE,)),
            pltpu.SemaphoreType.DMA((N_REMOTE,)),
        ],
        compiler_params=pltpu.CompilerParams(
            collective_id=0, has_side_effects=True, vmem_limit_bytes=60 * 1024 * 1024
        ),
        name="step",
    )(fragment, inputs, grad_kv, local_weight, global_weight, outer_moment, arrived)
    kv, gi, ln, gn, mn = pl.pallas_call(
        write_out,
        out_shape=tuple(jax.ShapeDtypeStruct(shape, dtype) for shape, dtype in shapes),
        in_specs=[vmem] * 5,
        out_specs=[hbm] * 5,
        scratch_shapes=[pltpu.SemaphoreType.DMA((5,))],
        compiler_params=pltpu.CompilerParams(vmem_limit_bytes=1024 * 1024),
        name="write",
    )(*(pltpu.with_memory_space_constraint(a, pltpu.VMEM) for a in held))
    return kv[None], gi[None], ln[None], gn, mn


def solution(mesh):
    return jax.shard_map(
        device_step,
        mesh=mesh,
        in_specs=(
            P("rep", "fsdp", None),
            P("rep", "fsdp", None),
            P("rep", "fsdp", None),
            P("fsdp", None),
            P("fsdp", None),
            P("fsdp", None),
            P(),
        ),
        out_specs=(
            P("rep", "fsdp", None),
            P("rep", "fsdp", None),
            P("rep", "fsdp", None),
            P("fsdp", None),
            P("fsdp", None),
        ),
        check_vma=False,
    )
```

```python
import jax
import jax.numpy as jnp
from jax import lax
from jax.experimental import pallas as pl
from jax.experimental.pallas import tpu as pltpu
from jax.sharding import PartitionSpec as P

inner_rate = 0.0001
outer_rate = 0.7
moment_keep = 0.9
merge_keep = 0.5

MESH = pl.DeviceIdType.MESH
F32, BF16, I16, I32 = jnp.float32, jnp.bfloat16, jnp.int16, jnp.int32
T = 192
D = 4096
KW = 512
H = 256
TOP = 32766.0


def exponent_for(bound):
    return jnp.ceil(8.0 * jnp.log2(jnp.maximum(bound, 1e-30) * (1.0 / TOP)))


def step_of(exponent):
    return jnp.exp2(exponent * 0.125)


def encode(values, inverse):
    return jnp.round(values * inverse).astype(I32).astype(I16)


def decode(codes, step):
    return codes.astype(I32).astype(F32) * step


def kernel(
    fragment_hbm, x_hbm, g_hbm, lw_hbm, gw_hbm, om_hbm, ar_hbm,
    kvo, gio, lno, gno, mno,
    xo, xs, go, gs, gt, lw, gw, om, ar, wa, wb, pt, top,
    c1s, c1r, a1os, a1or, a1xs, a1xr, a2os, a2or, a2xs, a2xr, a3os, a3or, a3xs, a3xr, a4s, a4r,
    acc, kva, gia,
    gr, gx, dl, ds, dr, fragment,
    lsem, ssem, rsem,
):
    r = lax.axis_index("rep")
    f = lax.axis_index("fsdp")
    z, y, x, c = f // 32, (f // 8) % 4, (f // 2) % 4, f % 2
    zx = 1 - z

    def dev(z_, y_, x_, c_):
        return (r, ((z_ * 4 + y_) * 4 + x_) * 2 + c_)

    sib = dev(z, y, x, 1 - c)
    zid = dev(zx, y, x, c)
    ids = ((lambda d: dev(z, y, (x + d) % 4, c)), (lambda d: dev(z, (y + d) % 4, x, c)))
    ring_id = ids
    line_id = (ids[1], ids[0])
    p = (x, y)
    q = (y, x)
    w = (wa, wb)
    cols = (slice(0, KW), slice(KW, 2 * KW))
    base = (0, H)
    own, oth = pl.ds(4 * z, 4), pl.ds(4 * zx, 4)
    turn = (1, 3)

    def chunk(g, plane, q_, p_):
        return plane * 16 + (q_ * 4 + p_ if g == 0 else p_ * 4 + q_)

    counts = [0, 0]
    sends = []

    def remote(src, dst, to):
        i = counts[0]
        counts[0] += 1
        cp = pltpu.make_async_remote_copy(
            src_ref=src, dst_ref=dst, send_sem=ssem.at[i], recv_sem=rsem.at[i], device_id=to, device_id_type=MESH
        )
        cp.start()
        sends.append(cp)
        return cp

    def same(ref, to):
        return remote(ref, ref, to)

    def local(src, dst):
        i = counts[1]
        counts[1] += 1
        cp = pltpu.make_async_copy(src, dst, lsem.at[i])
        cp.start()
        return cp

    partners = [sib, zid]
    partners += [ids[0](d) for d in (1, 2, 3)] + [ids[1](d) for d in (1, 2, 3)]
    partners += [((r + d) % 4, f) for d in (1, 2, 3)]
    barrier = pltpu.get_barrier_semaphore()
    for to in partners:
        pl.semaphore_signal(barrier, inc=1, device_id=to, device_id_type=MESH)

    lw_in = local(lw_hbm.at[0], lw)
    kva[...] = jnp.zeros_like(kva)
    gia[...] = jnp.zeros_like(gia)
    lw_in.wait()
    Q = D // 4
    go_in = local(g_hbm.at[0], go)
    xo_in = [local(x_hbm.at[0, :, pl.ds(Q * i, Q)], xo.at[:, pl.ds(Q * i, Q)]) for i in range(4)]
    gw_in = local(gw_hbm, gw)
    om_in = local(om_hbm, om)
    ar_in = local(ar_hbm, ar)
    fragment_in = local(fragment_hbm, fragment)
    for g in range(2):
        w[g][p[g], c, 4 * z + q[g]] = lw[:, cols[g]].astype(BF16)

    pl.semaphore_wait(barrier, len(partners))

    N = 3 * KW // 4
    sib_cols = pl.ds(pl.multiple_of((1 - c) * KW, KW), KW)
    my_cols = pl.ds(pl.multiple_of(c * KW, KW), KW)
    both = range(2)

    def tag(exponent):
        e16 = exponent.astype(I32).astype(I16)
        return jnp.concatenate([e16, e16], axis=0)

    def tag_of(rows):
        return step_of(rows.astype(I32).astype(F32)[0:8])

    def scale_of(bound):
        e = exponent_for(bound)
        return step_of(-e)[0:1], tag(e)

    def largest(values):
        return jnp.broadcast_to(jnp.max(values, axis=(0, 1), keepdims=True), (8, 128))

    def bound_of(g, plane, place):
        tops = [top[chunk(g, plane, k, place)] for k in range(4)]
        return largest(jnp.maximum(jnp.maximum(tops[0], tops[1]), jnp.maximum(tops[2], tops[3])))

    ag0, ag1, ag1x, ag2, ag2x, ag3, ag3x = ([None, None] for _ in range(7))
    cz, so, sx = ([{}, {}] for _ in range(3))

    def cross(g, place):
        return same(w[g].at[place, c, own, :, N:KW], zid)

    def share(g, place, plane):
        return same(w[g].at[place, c, plane], sib)

    def source(g, s):
        return (p[g] + turn[1 - s]) % 4

    def gather_z():
        for g in both:
            ag0[g] = same(w[g].at[p[g], c, 4 * z + q[g], :, 0:N], zid)

    def gather_line():
        for g in both:
            ag1[g] = [same(w[g].at[p[g], c, 4 * z + q[g]], line_id[g](d)) for d in (1, 2, 3)]

    def gather_line_x():
        for g in both:
            ag0[g].wait_recv()
            ag1x[g] = [same(w[g].at[p[g], c, 4 * zx + q[g], :, 0:N], line_id[g](d)) for d in (1, 2, 3)]

    def gather_ring():
        for g in both:
            for cp in ag1[g]:
                cp.wait_recv()
            ag2[g] = [same(w[g].at[p[g], c, own], ring_id[g](turn[s])) for s in both]

    def gather_ring_cross():
        for g in both:
            cz[g][0] = cross(g, p[g])
            so[g][0] = share(g, p[g], own)

    def gather_ring_x():
        for g in both:
            for cp in ag1x[g]:
                cp.wait_recv()
            ag2x[g] = [same(w[g].at[p[g], c, oth, :, 0:N], ring_id[g](turn[s])) for s in both]

    def gather_ring_x_share():
        for g in both:
            cz[g][0].wait_recv()
            sx[g][0] = share(g, p[g], oth)

    def gather_far():
        for g in both:
            ag3[g] = []
            for s in both:
                ag2[g][s].wait_recv()
                src = source(g, s)
                ag3[g].append(same(w[g].at[src, c, pl.ds(4 * z + 2 * s, 2)], ring_id[g](turn[s])))

    def gather_far_cross():
        for g in both:
            for s in both:
                cz[g][1 + s] = cross(g, source(g, s))
                so[g][1 + s] = share(g, source(g, s), own)

    def gather_far_x():
        for g in both:
            ag3x[g] = []
            for s in both:
                ag2x[g][s].wait_recv()
                src = source(g, s)
                ag3x[g].append(same(w[g].at[src, c, pl.ds(4 * zx + 2 * s, 2), :, 0:N], ring_id[g](turn[s])))

    def gather_far_x_share():
        for g in both:
            for s in both:
                cz[g][1 + s].wait_recv()
                sx[g][1 + s] = share(g, source(g, s), oth)

    def gather_end():
        for g in both:
            for s in both:
                ag3[g][s].wait_recv()
            cz[g][3] = cross(g, (p[g] + 2) % 4)
            so[g][3] = share(g, (p[g] + 2) % 4, own)

    def gather_end_x():
        for g in both:
            for s in both:
                ag3x[g][s].wait_recv()
            cz[g][3].wait_recv()
            sx[g][3] = share(g, (p[g] + 2) % 4, oth)

    def multiply(g, place, plane, copy):
        copy.wait_recv()
        parts = []
        rows = []
        lanes = []
        for k in range(4):
            parts += [w[g][place, 0, 4 * plane + k], w[g][place, 1, 4 * plane + k]]
            lanes.append(pl.ds(pl.multiple_of(chunk(g, plane, k, place) * 128, 128), 128))
            rows.append(xo[:, lanes[k]])
        tile = jnp.concatenate(parts, axis=0)
        kva[:, cols[g]] += jnp.dot(jnp.concatenate(rows, axis=1), tile, preferred_element_type=F32)
        back = lax.dot_general(go[:, cols[g]], tile, (((1,), (1,)), ((), ())), preferred_element_type=F32)
        for k in range(4):
            gia[:, lanes[k]] += back[:, 128 * k : 128 * (k + 1)]

    def multiply_own():
        for g in both:
            multiply(g, p[g], z, so[g][0])

    def multiply_own_x():
        for g in both:
            multiply(g, p[g], zx, sx[g][0])

    def multiply_near():
        for g in both:
            for s in both:
                multiply(g, source(g, s), z, so[g][1 + s])

    def multiply_near_x():
        for g in both:
            for s in both:
                multiply(g, source(g, s), zx, sx[g][1 + s])

    def multiply_far():
        for g in both:
            multiply(g, (p[g] + 2) % 4, z, so[g][3])

    def multiply_far_x():
        for g in both:
            multiply(g, (p[g] + 2) % 4, zx, sx[g][3])

    ex = {}

    def exchange():
        ex["g"] = remote(g_hbm.at[0, :, sib_cols], gs, sib)
        ex["x"] = [remote(x_hbm.at[0, :, pl.ds(Q * i, Q)], xs.at[:, pl.ds(Q * i, Q)], sib) for i in range(4)]

    def prepare():
        go_in.wait()
        gt[:, 0:T] = go[:, my_cols].T
        ex["g"].wait_recv()
        gt[:, T:] = gs[...].T

    def gradient(*pieces):
        for i in pieces:
            xo_in[i].wait()
            ex["x"][i].wait_recv()

            def block(n, carry):
                lanes = pl.ds(pl.multiple_of(Q * i + n * 256, 256), 256)
                rows = jnp.concatenate([xo[:, lanes], xs[:, lanes]], axis=0)
                part = jnp.dot(gt[...], rows, preferred_element_type=F32)
                pt[8 * i + 2 * n] = part[:, 0:128]
                pt[8 * i + 2 * n + 1] = part[:, 128:256]
                size = jnp.max(jnp.abs(part).reshape(64, 8, 256), axis=0)
                top[8 * i + 2 * n] = size[:, 0:128]
                top[8 * i + 2 * n + 1] = size[:, 128:256]
                return carry

            lax.fori_loop(0, 4, block, 0, unroll=True)

    stages = (2, 1, 3, 0)
    c1, rs1, rs1x, rs2, rs2x, rs3, rs3x, rs4 = ([None] * 4 for _ in range(8))
    extra = [None] * 4

    def cross_rows(i):
        d = stages[i]
        bound = jnp.maximum(bound_of(0, zx, (p[0] + d) % 4), bound_of(1, zx, (p[1] + d) % 4))
        inv, mark = scale_of(bound)
        for g in both:

            def enc(k, carry, g=g):
                part = pt[chunk(g, zx, k, (p[g] + d) % 4), pl.ds(base[g] + 192, 64)]
                c1s[i, pl.ds(pl.multiple_of(256 * g + 64 * k, 64), 64)] = encode(part, inv)
                return carry

            lax.fori_loop(0, 4, enc, 0)
        c1s[i, 512:528] = mark
        c1[i] = remote(c1s.at[i], c1r.at[i], zid)

    def crossed(i):
        c1[i].wait_recv()
        step = tag_of(c1r[i, 512:528])
        for g in both:

            def add(k, carry, g=g):
                at = chunk(g, z, k, (p[g] + stages[i]) % 4)
                rows = pl.ds(pl.multiple_of(256 * g + 64 * k, 64), 64)
                pt[at, pl.ds(base[g] + 192, 64)] += decode(c1r[i, rows], step[0:1])
                return carry

            lax.fori_loop(0, 4, add, 0)
        extra[stages[i]] = step * TOP

    def hop1(g, s, plane, half, buf, dst, more):
        inv, mark = scale_of(bound_of(g, plane, (p[g] + 2) % 4) + more)

        def enc(k, carry):
            part = pt[chunk(g, plane, k, (p[g] + 2) % 4), pl.ds(base[g] + half * s, half)]
            buf[pl.ds(pl.multiple_of(k * half, half), half)] = encode(part, inv)
            return carry

        lax.fori_loop(0, 4, enc, 0)
        buf[4 * half : 4 * half + 16] = mark
        return remote(buf, dst, ring_id[g](turn[s]))

    def scatter1_x():
        for g in both:
            rs1x[g] = [hop1(g, s, zx, 96, a1xs.at[g, s], a1xr.at[g, s], 0.0) for s in both]

    def scatter1():
        for g in both:
            rs1[g] = [hop1(g, s, z, 128, a1os.at[g, s], a1or.at[g, s], extra[2]) for s in both]

    def hop2(g, s, plane, half, copy, got, buf, dst, more):
        copy.wait_recv()
        step = tag_of(got[4 * half : 4 * half + 16])
        inv, mark = scale_of(more + bound_of(g, plane, (p[g] + turn[s]) % 4) + step * TOP)
        step = step[0:1]

        def enc(k, carry):
            at = chunk(g, plane, k, (p[g] + turn[s]) % 4)
            fed = pt[at, pl.ds(base[g] + half * s, half)] + decode(got[pl.ds(pl.multiple_of(k * half, half), half)], step)
            plain = pt[at, pl.ds(base[g] + half * (1 - s), half)]
            buf[pl.ds(pl.multiple_of(2 * k * half + half * s, half), half)] = encode(fed, inv)
            buf[pl.ds(pl.multiple_of(2 * k * half + half * (1 - s), half), half)] = encode(plain, inv)
            return carry

        lax.fori_loop(0, 4, enc, 0)
        buf[8 * half : 8 * half + 16] = mark
        return remote(buf, dst, ring_id[g](turn[s]))

    def scatter2_x():
        for g in both:
            rs2x[g] = [
                hop2(g, s, zx, 96, rs1x[g][s], a1xr.at[g, s], a2xs.at[g, s], a2xr.at[g, s], 0.0) for s in both
            ]

    def scatter2():
        for g in both:
            rs2[g] = [
                hop2(g, s, z, 128, rs1[g][s], a1or.at[g, s], a2os.at[g, s], a2or.at[g, s], extra[turn[s]]) for s in both
            ]

    def hop3(g, plane, rows, copies, got, buf, dst):
        steps = []
        for s in both:
            copies[s].wait_recv()
            steps.append(tag_of(got[s, 4 * rows : 4 * rows + 16])[0:1])
        size = jnp.zeros((8, 128), F32)
        for d in (1, 2, 3, 0):
            k = (q[g] + d) % 4
            part = pl.ds(pl.multiple_of(k * rows, rows), rows)
            at = chunk(g, plane, k, p[g])
            total = pt[at, pl.ds(base[g], rows)] + decode(got[0, part], steps[0]) + decode(got[1, part], steps[1])
            pt[at, pl.ds(base[g], rows)] = total
            if d:
                size = jnp.maximum(size, jnp.max(jnp.abs(total).reshape(rows // 8, 8, 128), axis=0))
        inv, mark = scale_of(largest(size))
        sent = []
        for d in (1, 2, 3):
            at = chunk(g, plane, (q[g] + d) % 4, p[g])
            buf[d - 1, 0:rows] = encode(pt[at, pl.ds(base[g], rows)], inv)
            buf[d - 1, rows : rows + 16] = mark
            sent.append(remote(buf.at[d - 1], dst.at[d - 1], line_id[g](d)))
        return sent

    def scatter3_x():
        for g in both:
            rs3x[g] = hop3(g, zx, 192, rs2x[g], a2xr.at[g], a3xs.at[g], a3xr.at[g])

    def scatter3():
        for g in both:
            rs3[g] = hop3(g, z, 256, rs2[g], a2or.at[g], a3os.at[g], a3or.at[g])

    def scatter4():
        for g in both:
            part = pt[chunk(g, zx, q[g], p[g]), pl.ds(base[g], 192)]
            for j in range(3):
                rs3x[g][j].wait_recv()
                part = part + decode(a3xr[g, j, 0:192], tag_of(a3xr[g, j, 192:208])[0:1])
            inv, mark = scale_of(largest(jnp.abs(part)))
            a4s[g, 0:192] = encode(part, inv)
            a4s[g, 192:208] = mark
            rs4[g] = remote(a4s.at[g], a4r.at[g], zid)

    def scatter_end():
        for g in both:
            part = pt[chunk(g, z, q[g], p[g]), pl.ds(base[g], 256)]
            for j in range(3):
                rs3[g][j].wait_recv()
                part = part + decode(a3or[g, j, 0:256], tag_of(a3or[g, j, 256:272])[0:1])
            acc[pl.ds(base[g], 256)] = part
            rs4[g].wait_recv()
            acc[pl.ds(base[g], 192)] += decode(a4r[g, 0:192], tag_of(a4r[g, 192:208])[0:1])
            gr[:, pl.ds(base[g], 256)] = acc[pl.ds(base[g], 256)].T
        ex["gx"] = remote(gr.at[pl.ds(pl.multiple_of((1 - c) * 64, 64), 64)], gx, sib)

    def is_first():
        return fragment[0] % 2 == 0

    def delta():
        gw_in.wait()
        fragment_in.wait()
        first = is_first()
        dl[...] = jnp.where(first, gw[:, 0:KW] - lw[:, 0:KW], gw[:, KW:] - lw[:, KW:])
        ed = exponent_for(largest(jnp.abs(dl[...])))
        ds[0:64] = encode(dl[...], jnp.concatenate([step_of(-ed)[0:1]] * 4, axis=1))
        ds[64:80] = jnp.concatenate([tag(ed)] * 4, axis=1)

    def replicas():
        ex["rep"] = [remote(ds, dr.at[d - 1], ((r + d) % 4, f)) for d in (1, 2, 3)]

    def outer():
        om_in.wait()
        first = is_first()
        mean_delta = dl[...]
        for j in range(3):
            ex["rep"][j].wait_recv()
            step = tag_of(dr[j, 64:80])
            mean_delta = mean_delta + decode(dr[j, 0:64], step[0:1])
        mean_delta = mean_delta * 0.25
        moment_new = moment_keep * jnp.where(first, om[:, 0:KW], om[:, KW:]) + mean_delta
        global_new = jnp.where(first, gw[:, 0:KW], gw[:, KW:]) - outer_rate * (mean_delta + moment_keep * moment_new)
        for h in both:
            sel = first if h == 0 else jnp.logical_not(first)
            mno[:, cols[h]] = jnp.where(sel, moment_new, om[:, cols[h]])
            gno[:, cols[h]] = jnp.where(sel, global_new, gw[:, cols[h]])

    def half_out(plane):
        lanes = pl.ds(pl.multiple_of(plane * (D // 2), D // 2), D // 2)
        gio[:, lanes] = gia[:, lanes].astype(BF16)

    def products_own():
        half_out(z)

    def products_x():
        half_out(zx)
        kvo[...] = kva[...].astype(BF16)

    def inner_out():
        ar_in.wait()
        ex["gx"].wait_recv()
        first = is_first()
        here = gr[pl.ds(pl.multiple_of(c * 64, 64), 64)]
        there = gx[...]
        for h in both:
            gradient_h = jnp.where(c == h, here, there)
            inner = lw[:, cols[h]] - inner_rate * gradient_h
            sel = first if h == 0 else jnp.logical_not(first)
            merged = merge_keep * inner + (1.0 - merge_keep) * ar[...]
            lno[:, cols[h]] = jnp.where(sel, merged, inner)

    gather_z()
    gather_line()
    exchange()
    prepare()
    gather_line_x()
    gather_ring()
    gather_ring_cross()
    gradient(0,1,2,3)
    for i in range(4):
        cross_rows(i)
    scatter1_x()
    gather_ring_x()
    crossed(0)
    scatter1()
    gather_ring_x_share()
    scatter2_x()
    delta()
    replicas()
    multiply_own()
    crossed(1)
    crossed(2)
    scatter2()
    gather_far()
    gather_far_cross()
    multiply_own_x()
    scatter3_x()
    gather_far_x()
    gather_far_x_share()
    crossed(3)
    scatter3()
    outer()
    multiply_near()
    gather_end()
    scatter4()
    multiply_near_x()
    multiply_far()
    products_own()
    gather_end_x()
    scatter_end()
    multiply_far_x()
    products_x()
    inner_out()

    for cp in sends:
        cp.wait_send()
    assert counts[0] <= N_REMOTE and counts[1] <= N_LOCAL


def write_out(*refs):
    sem = refs[10]
    copies = [pltpu.make_async_copy(refs[i], refs[5 + i], sem.at[i]) for i in range(5)]
    for cp in copies:
        cp.start()
    for cp in copies:
        cp.wait()


N_REMOTE = 120
N_LOCAL = 16


def device_step(inputs, grad_kv, local_weight, global_weight, outer_moment, arrived, fragment):
    hbm = pl.BlockSpec(memory_space=pltpu.HBM)
    vmem = pl.BlockSpec(memory_space=pltpu.VMEM)
    R = D // 64
    V = pltpu.VMEM
    shapes = (((T, 2 * KW), BF16), ((T, D), BF16), ((R, 2 * KW), F32), ((R, 2 * KW), F32), ((R, 2 * KW), F32))
    held = pl.pallas_call(
        kernel,
        out_shape=tuple(V(shape, dtype) for shape, dtype in shapes),
        in_specs=[hbm] * 7,
        out_specs=[vmem] * 5,
        scratch_shapes=[
            V((T, D), BF16), V((T, D), BF16),
            V((T, 2 * KW), BF16), V((T, KW), BF16), V((KW, 2 * T), BF16),
            V((R, 2 * KW), F32), V((R, 2 * KW), F32), V((R, 2 * KW), F32), V((R, KW), F32),
            V((4, 2, 8, R, KW), BF16), V((4, 2, 8, R, KW), BF16),
            V((32, KW, 128), F32), V((32, 8, 128), F32),
            V((4, 528, 128), I16), V((4, 528, 128), I16),
            V((2, 2, 528, 128), I16), V((2, 2, 528, 128), I16),
            V((2, 2, 400, 128), I16), V((2, 2, 400, 128), I16),
            V((2, 2, 1040, 128), I16), V((2, 2, 1040, 128), I16),
            V((2, 2, 784, 128), I16), V((2, 2, 784, 128), I16),
            V((2, 3, 272, 128), I16), V((2, 3, 272, 128), I16),
            V((2, 3, 208, 128), I16), V((2, 3, 208, 128), I16),
            V((2, 208, 128), I16), V((2, 208, 128), I16),
            V((KW, 128), F32), V((T, 2 * KW), F32), V((T, D), F32),
            V((128, KW), F32), V((R, KW), F32), V((R, KW), F32),
            V((R + 16, KW), I16), V((3, R + 16, KW), I16),
            pltpu.SMEM((1,), I32),
            pltpu.SemaphoreType.DMA((N_LOCAL,)),
            pltpu.SemaphoreType.DMA((N_REMOTE,)),
            pltpu.SemaphoreType.DMA((N_REMOTE,)),
        ],
        compiler_params=pltpu.CompilerParams(
            collective_id=0, has_side_effects=True, vmem_limit_bytes=60 * 1024 * 1024
        ),
        name="step",
    )(fragment, inputs, grad_kv, local_weight, global_weight, outer_moment, arrived)
    kv, gi, ln, gn, mn = pl.pallas_call(
        write_out,
        out_shape=tuple(jax.ShapeDtypeStruct(shape, dtype) for shape, dtype in shapes),
        in_specs=[vmem] * 5,
        out_specs=[hbm] * 5,
        scratch_shapes=[pltpu.SemaphoreType.DMA((5,))],
        compiler_params=pltpu.CompilerParams(vmem_limit_bytes=1024 * 1024),
        name="write",
    )(*(pltpu.with_memory_space_constraint(a, pltpu.VMEM) for a in held))
    return kv[None], gi[None], ln[None], gn, mn


def solution(mesh):
    return jax.shard_map(
        device_step,
        mesh=mesh,
        in_specs=(
            P("rep", "fsdp", None),
            P("rep", "fsdp", None),
            P("rep", "fsdp", None),
            P("fsdp", None),
            P("fsdp", None),
            P("fsdp", None),
            P(),
        ),
        out_specs=(
            P("rep", "fsdp", None),
            P("rep", "fsdp", None),
            P("rep", "fsdp", None),
            P("fsdp", None),
            P("fsdp", None),
        ),
        check_vma=False,
    )
```
